32 devices in a mesh: row: 8 (over y, x, core), col: 4 (over z).
Axes of the slice: x: 2, y: 2, z: 4, core: 2. Of those that a mesh axis runs over, the one named last changes fastest.
Arguments:
- pair: bfloat16 [512, 512, 128], P('row', 'col'), may hold values from -6 to 6
- ln_gain: float32 [128], replicated, may hold values from 0.1 to 1.9
- ln_bias: float32 [128], replicated, may hold values from -3 to 3
- gate_weight: bfloat16 [128, 512], replicated, may hold values from -0.5 to 0.5
- up_weight: bfloat16 [128, 512], replicated, may hold values from -0.5 to 0.5
- out_weight: bfloat16 [512, 128], replicated, may hold values from -0.25 to 0.25
- head_weight: bfloat16 [128, 64], replicated, may hold values from -1 to 1
- targets: int32 [512, 512], P(('row', 'col')), may hold values from 0 to 63
- pair_mask: int32 [512, 512], P(('row', 'col')), may hold values 0 or 1
Outputs:
- pair_out: bfloat16 [512, 512, 128], P('row', 'col')
- loss: float32 [], replicated
- grad_gain: float32 [128], replicated
- grad_bias: float32 [128], replicated
- grad_gate: float32 [128, 512], replicated
- grad_up: float32 [128, 512], replicated
- grad_out: float32 [512, 128], replicated
- grad_head: float32 [128, 64], replicated
The draws below stay inside these ranges and needn't reach their ends.
All inputs are finite; a program needn't handle non-finite values. No bound on the sum of `pair_mask` on one device may be relied on, other than what follows from the above.
Results may differ from the reference program's by a relative error of at most 0.001.
The reference program's roundings to bfloat16 on the way (of `normed`, `hidden`, `half`, `grad_logits`, `grad_flip` and `grad_pair`) count: a program that leaves them out, or rounds other values in their place, can miss the bound.
Values may be sent and summed in bfloat16 or wider, within the bound.
A program may use at most 64 MiB of HBM per device.

```python
import math
import jax
import jax.numpy as jnp
from jax import lax

C_Z = 128
C_HID = 512
BINS = 64
N_TOK = 512


def plant(array, key, smallest, largest):
    place = [jax.random.randint(jax.random.fold_in(key, axis), (), 0, length) for axis, length in enumerate(array.shape)]
    widest = array.shape.index(max(array.shape))
    neighbour = place[:widest] + [(place[widest] + 1) % array.shape[widest]] + place[widest + 1:]
    return array.at[tuple(place)].set(smallest).at[tuple(neighbour)].set(largest)


def steps_of(own_key, dims, split, smallest, high):
    loudness = 1.0
    for position, parts in split:
        steps = jax.random.uniform(jax.random.fold_in(jax.random.fold_in(own_key, 6), position), (parts,), jnp.float32, smallest / len(split), high / len(split))
        loudness = loudness * jnp.repeat(jnp.exp(steps), dims[position] // parts).reshape((-1,) + (1,) * (len(dims) - 1 - position))
    return loudness


def bell_draw(key, extent, scale, reach, cuts=(), kind=jnp.bfloat16):
    factor_of = steps_of(key, extent, cuts, -0.22, 0.18) if cuts else 1.0
    result = jax.random.normal(key, extent, jnp.float32) * scale * factor_of
    return jnp.minimum(jnp.maximum(result, -reach), reach).astype(kind)


def setup_inputs(seed: int = 0) -> dict:
    streams_of = jax.random.split(jax.random.key(seed), 10)
    return {
        "pair": bell_draw(streams_of[0], (N_TOK, N_TOK, C_Z), 1.0, 6.0, ((0, 8), (1, 4))),
        "ln_gain": jnp.clip(1.0 + 0.18 * jax.random.normal(streams_of[1], (C_Z,), jnp.float32), 0.1, 1.9),
        "ln_bias": bell_draw(streams_of[2], (C_Z,), 0.5, 3.0, (), jnp.float32),
        "gate_weight": bell_draw(streams_of[3], (C_Z, C_HID), C_Z ** -0.5, 0.5),
        "up_weight": bell_draw(streams_of[4], (C_Z, C_HID), C_Z ** -0.5, 0.5),
        "out_weight": bell_draw(streams_of[5], (C_HID, C_Z), C_HID ** -0.5, 0.25),
        "head_weight": bell_draw(streams_of[6], (C_Z, BINS), (C_Z // 4) ** -0.5, 1.0),
        "targets": plant(jax.random.randint(streams_of[7], (N_TOK, N_TOK), 0, BINS), jax.random.fold_in(streams_of[7], 1), 0, BINS - 1).astype(jnp.int32),
        "pair_mask": plant((jax.random.randint(streams_of[8], (N_TOK, N_TOK), 0, 4) < 3).astype(jnp.int32), jax.random.fold_in(streams_of[8], 1), 0, 1),
    }


EPSILON = 1e-05

def normalize(rows_in, ln_gain, ln_bias):
    values = rows_in.astype(jnp.float32)
    centered = values - lax.optimization_barrier(jnp.mean(values, axis=-1, keepdims=True))
    variance = lax.optimization_barrier(jnp.mean(centered * centered, axis=-1, keepdims=True))
    unit_rows = centered * lax.rsqrt(variance + EPSILON)
    normed = (unit_rows * ln_gain + ln_bias).astype(jnp.bfloat16)
    return (unit_rows, normed)

def inner(left, right):
    return lax.dot_general(left, right, (((0,), (0,)), ((), ())), preferred_element_type=jnp.float32)

def advance(rows_in, ln_gain, ln_bias, gate_weight, up_weight, out_weight):
    unit_rows, normed = normalize(rows_in, ln_gain, ln_bias)
    gate_pre = jnp.dot(normed, gate_weight, preferred_element_type=jnp.float32)
    up_pre = jnp.dot(normed, up_weight, preferred_element_type=jnp.float32)
    hidden = (jax.nn.silu(gate_pre) * up_pre).astype(jnp.bfloat16)
    update = jnp.dot(hidden, out_weight, preferred_element_type=jnp.float32)
    return (rows_in.astype(jnp.float32) + update).astype(jnp.bfloat16)

def retreat(totals, rows_in, grad_rows, ln_gain, ln_bias, gate_weight, up_weight, out_weight):
    unit_rows, normed = normalize(rows_in, ln_gain, ln_bias)
    gate_pre = jnp.dot(normed, gate_weight, preferred_element_type=jnp.float32)
    up_pre = jnp.dot(normed, up_weight, preferred_element_type=jnp.float32)
    squashed = jax.nn.sigmoid(gate_pre)
    silu_val = gate_pre * squashed
    hidden = (silu_val * up_pre).astype(jnp.bfloat16)
    grad_hidden = jnp.dot(grad_rows, out_weight.T, preferred_element_type=jnp.float32)
    grad_gate_pre = (grad_hidden * up_pre * squashed * (1.0 + gate_pre * (1.0 - squashed))).astype(jnp.bfloat16)
    grad_up_pre = (grad_hidden * silu_val).astype(jnp.bfloat16)
    grad_normed = jnp.dot(grad_gate_pre, gate_weight.T, preferred_element_type=jnp.float32) + jnp.dot(grad_up_pre, up_weight.T, preferred_element_type=jnp.float32)
    sum_gain, sum_bias, sum_gate, sum_up, sum_out = totals
    return (sum_gain + lax.optimization_barrier(jnp.sum(grad_normed * unit_rows, axis=0)), sum_bias + lax.optimization_barrier(jnp.sum(grad_normed, axis=0)), sum_gate + inner(normed, grad_gate_pre), sum_up + inner(normed, grad_up_pre), sum_out + inner(hidden, grad_rows))

def reference(pair, ln_gain, ln_bias, gate_weight, up_weight, out_weight, head_weight, targets, pair_mask):
    tokens = N_TOK
    width = pair.shape[-1]
    block_rows = math.gcd(tokens, 16)
    count = tokens // block_rows
    blocks = pair.reshape(count, block_rows * tokens, width)

    def forward_one(rows_in):
        return advance(rows_in, ln_gain, ln_bias, gate_weight, up_weight, out_weight)
    pair_out = lax.map(forward_one, blocks).reshape(pair.shape)
    half = jnp.dot(pair_out, head_weight, preferred_element_type=jnp.float32).astype(jnp.bfloat16)
    logits = half.astype(jnp.float32) + jnp.swapaxes(half, 0, 1).astype(jnp.float32)
    bins = logits.shape[-1]
    one_hot = (targets[..., None] == jnp.arange(bins, dtype=jnp.int32)).astype(jnp.float32)
    log_total = jnp.log(lax.optimization_barrier(jnp.sum(jnp.exp(logits), axis=-1)))
    weights_mask = pair_mask.astype(jnp.float32)
    nll = log_total - lax.optimization_barrier(jnp.sum(logits * one_hot, axis=-1))
    loss = jnp.sum(weights_mask * nll) / (tokens * tokens)
    soft_probs = jnp.exp(logits - log_total[..., None])
    grad_logits = (weights_mask[..., None] * (soft_probs - one_hot) / tokens).astype(jnp.bfloat16)
    grad_flip = jnp.swapaxes(grad_logits, 0, 1)
    flat_out = pair_out.reshape(-1, width)
    grad_head = inner(flat_out, grad_logits.reshape(-1, bins)) + inner(flat_out, grad_flip.reshape(-1, bins))
    head_back = head_weight.T
    grad_pair = (jnp.dot(grad_logits, head_back, preferred_element_type=jnp.float32) + jnp.dot(grad_flip, head_back, preferred_element_type=jnp.float32)).astype(jnp.bfloat16)
    grad_blocks = grad_pair.reshape(count, block_rows * tokens, width)
    hidden_width = gate_weight.shape[1]
    start = (jnp.zeros((width,), jnp.float32), jnp.zeros((width,), jnp.float32), jnp.zeros((width, hidden_width), jnp.float32), jnp.zeros((width, hidden_width), jnp.float32), jnp.zeros((hidden_width, width), jnp.float32))

    def backward_one(totals, inputs):
        return (retreat(totals, inputs[0], inputs[1], ln_gain, ln_bias, gate_weight, up_weight, out_weight), None)
    totals, unused = lax.scan(backward_one, start, (blocks, grad_blocks))
    return (pair_out, loss, totals[0], totals[1], totals[2], totals[3], totals[4], grad_head)
```

```python
import functools
import math

import jax
import jax.numpy as jnp
from jax import lax
from jax.experimental import pallas as pl
from jax.experimental.pallas import tpu as pltpu
from jax.sharding import PartitionSpec as P

EPSILON = 1e-05


def normalize(rows_in, ln_gain, ln_bias):
    values = rows_in.astype(jnp.float32)
    centered = values - jnp.mean(values, axis=-1, keepdims=True)
    variance = jnp.mean(centered * centered, axis=-1, keepdims=True)
    unit_rows = centered * lax.rsqrt(variance + EPSILON)
    normed = (unit_rows * ln_gain + ln_bias).astype(jnp.bfloat16)
    return (unit_rows, normed)


def inner(left, right):
    return lax.dot_general(
        left, right, (((0,), (0,)), ((), ())), preferred_element_type=jnp.float32
    )


def advance(rows_in, ln_gain, ln_bias, gate_weight, up_weight, out_weight):
    unit_rows, normed = normalize(rows_in, ln_gain, ln_bias)
    gate_pre = jnp.dot(normed, gate_weight, preferred_element_type=jnp.float32)
    up_pre = jnp.dot(normed, up_weight, preferred_element_type=jnp.float32)
    hidden = (jax.nn.silu(gate_pre) * up_pre).astype(jnp.bfloat16)
    update = jnp.dot(hidden, out_weight, preferred_element_type=jnp.float32)
    return (rows_in.astype(jnp.float32) + update).astype(jnp.bfloat16)


def retreat(totals, rows_in, grad_rows, ln_gain, ln_bias, gate_weight, up_weight, out_weight):
    unit_rows, normed = normalize(rows_in, ln_gain, ln_bias)
    gate_pre = jnp.dot(normed, gate_weight, preferred_element_type=jnp.float32)
    up_pre = jnp.dot(normed, up_weight, preferred_element_type=jnp.float32)
    squashed = jax.nn.sigmoid(gate_pre)
    silu_val = gate_pre * squashed
    hidden = (silu_val * up_pre).astype(jnp.bfloat16)
    grad_hidden = jnp.dot(grad_rows, out_weight.T, preferred_element_type=jnp.float32)
    grad_gate_pre = (grad_hidden * up_pre * squashed * (1.0 + gate_pre * (1.0 - squashed))).astype(
        jnp.bfloat16
    )
    grad_up_pre = (grad_hidden * silu_val).astype(jnp.bfloat16)
    grad_normed = jnp.dot(
        grad_gate_pre, gate_weight.T, preferred_element_type=jnp.float32
    ) + jnp.dot(grad_up_pre, up_weight.T, preferred_element_type=jnp.float32)
    sum_gain, sum_bias, sum_gate, sum_up, sum_out = totals
    return (
        sum_gain + jnp.sum(grad_normed * unit_rows, axis=0),
        sum_bias + jnp.sum(grad_normed, axis=0),
        sum_gate + inner(normed, grad_gate_pre),
        sum_up + inner(normed, grad_up_pre),
        sum_out + inner(hidden, grad_rows),
    )


def loss_terms(logits, targets, pair_mask):
    bins = logits.shape[-1]
    one_hot = (targets[..., None] == jnp.arange(bins, dtype=jnp.int32)).astype(jnp.float32)
    log_total = jnp.log(jnp.sum(jnp.exp(logits), axis=-1))
    weights_mask = pair_mask.astype(jnp.float32)
    loss_part = jnp.sum(weights_mask * (log_total - jnp.sum(logits * one_hot, axis=-1)))
    soft_probs = jnp.exp(logits - log_total[..., None])
    return (loss_part, soft_probs)


def grad_from(soft_probs, targets, pair_mask, tokens):
    bins = soft_probs.shape[-1]
    one_hot = (targets[..., None] == jnp.arange(bins, dtype=jnp.int32)).astype(jnp.float32)
    weights_mask = pair_mask.astype(jnp.float32)
    return (weights_mask[..., None] * (soft_probs - one_hot) / tokens).astype(jnp.bfloat16)


def flip_bit(axis, bit):
    place = lax.axis_index(axis)
    mine = lax.rem(lax.div(place, bit), 2)
    return mine, place + bit - 2 * bit * mine


def total_kernel(bits, parts, shapes, *refs):
    count = len(shapes)
    ins, outs = refs[:count], refs[count : 2 * count]
    acc, full, send_sem, recv_sem = refs[2 * count : 2 * count + 4]
    landing = refs[2 * count + 4 :]
    steps = len(bits)
    barrier = pltpu.get_barrier_semaphore()
    sides = []
    for axis, bit in bits:
        mine, partner = flip_bit(axis, bit)
        sides.append((mine, {axis: partner}))
        pl.semaphore_signal(
            barrier, inc=1, device_id={axis: partner}, device_id_type=pl.DeviceIdType.MESH
        )
    row = 0
    for ref, shape in zip(ins, shapes):
        for left in range(0, shape[1], 128):
            wide = min(128, shape[1] - left)
            acc[row : row + shape[0], :wide] = ref[:, left : left + wide]
            if wide < 128:
                acc[row : row + shape[0], wide:] = jnp.zeros((shape[0], 128 - wide), jnp.float32)
            row += shape[0]
    if row < acc.shape[0]:
        acc[row:, :] = jnp.zeros((acc.shape[0] - row, 128), jnp.float32)
    pl.semaphore_wait(barrier, steps)

    def push(part, slot, source, target, device):
        return pltpu.make_async_remote_copy(
            src_ref=source,
            dst_ref=target,
            send_sem=send_sem.at[part, slot],
            recv_sem=recv_sem.at[part, slot],
            device_id=device,
            device_id_type=pl.DeviceIdType.MESH,
        )

    spots = [(base, size) for base, size, order in parts]
    trail = [[] for part in parts]
    for step in range(steps):
        moves = []
        for index, (base, size, order) in enumerate(parts):
            mine, device = sides[order[step]]
            start, length = spots[index]
            land = landing[index * steps + step]
            if step < steps - 1:
                length //= 2
                keep = pl.multiple_of(start + mine * length, 8)
                give = pl.multiple_of(start + (1 - mine) * length, 8)
                trail[index].append((keep, length, order[step]))
            else:
                keep = give = start
            copy = push(index, step, acc.at[pl.ds(give, length)], land, device)
            copy.start()
            moves.append((copy, keep, length, land))
            spots[index] = (keep, length)
        for copy, keep, length, land in moves:
            copy.wait()
            into = acc if step < steps - 1 else full
            into[pl.ds(keep, length), :] = acc[pl.ds(keep, length), :] + land[...]
    for step in range(steps - 2, -1, -1):
        moves = []
        for index, (base, size, order) in enumerate(parts):
            keep, length, which = trail[index][step]
            spot = full.at[pl.ds(keep, length)]
            copy = push(index, 2 * steps - 2 - step, spot, spot, sides[which][1])
            copy.start()
            moves.append(copy)
        for copy in moves:
            copy.wait()
    row = 0
    for ref, shape in zip(outs, shapes):
        for left in range(0, shape[1], 128):
            wide = min(128, shape[1] - left)
            ref[:, left : left + wide] = full[row : row + shape[0], :wide]
            row += shape[0]


def total(arrays):
    bits = []
    for axis in ("row", "col"):
        size, bit = lax.axis_size(axis), 1
        if size & (size - 1):
            return lax.psum(arrays, ("row", "col"))
        while bit < size:
            bits.append((axis, bit))
            bit *= 2
    if len(bits) < 2:
        return lax.psum(arrays, ("row", "col"))
    shapes = tuple(array.shape for array in arrays)
    rows = sum(shape[0] * (-(-shape[1] // 128)) for shape in shapes)
    steps = len(bits)
    grain = 8 * 2 ** (steps - 1)
    grains = -(-rows // grain)
    inner_bits = list(range(1, steps - 1))
    turns = max(1, min(3, len(inner_bits), grains))
    parts, base = [], 0
    for turn in range(turns):
        size = grain * (grains // turns + (turn < grains % turns))
        order = [0] + inner_bits[turn:] + inner_bits[:turn] + [steps - 1]
        parts.append((base, size, order))
        base += size
    landing = []
    for base_at, size, order in parts:
        for step in range(steps):
            landing.append(
                pltpu.VMEM((size >> min(step + 1, steps - 1), 128), jnp.float32)
            )
    vmem = pl.BlockSpec(memory_space=pltpu.VMEM)
    return pl.pallas_call(
        functools.partial(total_kernel, bits, parts, shapes),
        out_shape=[jax.ShapeDtypeStruct(shape, jnp.float32) for shape in shapes],
        in_specs=[vmem] * len(shapes),
        out_specs=[vmem] * len(shapes),
        scratch_shapes=[
            pltpu.VMEM((base, 128), jnp.float32),
            pltpu.VMEM((base, 128), jnp.float32),
            pltpu.SemaphoreType.DMA((turns, 2 * steps - 1)),
            pltpu.SemaphoreType.DMA((turns, 2 * steps - 1)),
        ]
        + landing,
        compiler_params=pltpu.CompilerParams(
            collective_id=0, has_side_effects=True, vmem_limit_bytes=32 * 1024 * 1024
        ),
        name="total",
    )(*arrays)


def mirror(half_tile):
    across, down = lax.axis_size("row"), lax.axis_size("col")
    fold = across // down
    edge, bins = half_tile.shape[0], half_tile.shape[2]
    place, column = lax.axis_index("row"), lax.axis_index("col")
    flipped = jnp.zeros_like(half_tile)
    for turn in range(fold):
        sub = lax.rem(place + turn, fold)
        block = lax.dynamic_slice(half_tile, (0, sub * edge, 0), (edge, edge, bins))
        packed = jnp.concatenate([block[: edge // 2], block[edge // 2 :]], axis=-1)
        pairs = [
            (r * down + c, (c * fold + (r + turn) % fold) * down + r // fold)
            for r in range(across)
            for c in range(down)
        ]
        came = lax.ppermute(packed, ("row", "col"), pairs)
        whole = jnp.concatenate([came[..., :bins], came[..., bins:]], axis=0)
        spot = lax.rem(place + turn * (fold - 1), fold)
        flipped = lax.dynamic_update_slice(
            flipped, jnp.swapaxes(whole, 0, 1), (0, spot * edge, 0)
        )
    return flipped


def shards(
    pair, ln_gain, ln_bias, gate_weight, up_weight, out_weight, head_weight, targets, pair_mask
):
    rows_tile, cols_tile, width = pair.shape
    tokens = cols_tile * lax.axis_size("col")
    block_rows = math.gcd(rows_tile, max(1, 2048 // cols_tile))
    count = rows_tile // block_rows
    blocks = pair.reshape(count, block_rows * cols_tile, width)

    def forward_one(rows_in):
        return advance(rows_in, ln_gain, ln_bias, gate_weight, up_weight, out_weight)

    pair_out = lax.map(forward_one, blocks).reshape(pair.shape)
    half_tile = jnp.dot(pair_out, head_weight, preferred_element_type=jnp.float32).astype(
        jnp.bfloat16
    )
    half_flip = mirror(half_tile)
    code = jnp.where(pair_mask > 0, targets, -1)
    codes = lax.all_gather(code, ("row", "col"), axis=0, tiled=True)
    top, side = lax.axis_index("row") * rows_tile, lax.axis_index("col") * cols_tile
    target_tile = lax.dynamic_slice(codes, (top, side), (rows_tile, cols_tile))
    target_turn = lax.dynamic_slice(codes, (side, top), (cols_tile, rows_tile)).T
    mask_tile = (target_tile >= 0).astype(jnp.int32)
    mask_turn = (target_turn >= 0).astype(jnp.int32)
    logits = half_tile.astype(jnp.float32) + half_flip.astype(jnp.float32)
    loss_part, soft_probs = loss_terms(logits, target_tile, mask_tile)
    tile_grad = grad_from(soft_probs, target_tile, mask_tile, tokens)
    tile_flip = grad_from(soft_probs, target_turn, mask_turn, tokens)
    bins = head_weight.shape[1]
    flat_out = pair_out.reshape(-1, width)
    grad_head = inner(flat_out, tile_grad.reshape(-1, bins)) + inner(
        flat_out, tile_flip.reshape(-1, bins)
    )
    head_back = head_weight.T
    grad_pair = (
        jnp.dot(tile_grad, head_back, preferred_element_type=jnp.float32)
        + jnp.dot(tile_flip, head_back, preferred_element_type=jnp.float32)
    ).astype(jnp.bfloat16)
    grad_blocks = grad_pair.reshape(count, block_rows * cols_tile, width)
    hidden_width = gate_weight.shape[1]
    start = (
        jnp.zeros((width,), jnp.float32),
        jnp.zeros((width,), jnp.float32),
        jnp.zeros((width, hidden_width), jnp.float32),
        jnp.zeros((width, hidden_width), jnp.float32),
        jnp.zeros((hidden_width, width), jnp.float32),
    )

    def backward_one(totals, inputs):
        return (
            retreat(
                totals, inputs[0], inputs[1], ln_gain, ln_bias, gate_weight, up_weight, out_weight
            ),
            None,
        )

    totals, unused = lax.scan(backward_one, start, (blocks, grad_blocks))
    few = jnp.concatenate(
        [
            totals[0][None],
            totals[1][None],
            jnp.broadcast_to(loss_part, (1, width)),
            jnp.zeros((5, width), jnp.float32),
        ]
    )
    gate_sum, up_sum, out_sum, head_sum, few = total([totals[2], totals[3], totals[4], grad_head, few])
    loss = few[2, 0] / (tokens * tokens)
    return (pair_out, loss, few[0], few[1], gate_sum, up_sum, out_sum, head_sum)


def solution(mesh):
    placed = (
        P("row", "col", None),
        P(),
        P(),
        P(),
        P(),
        P(),
        P(),
        P(("row", "col"), None),
        P(("row", "col"), None),
    )
    return jax.shard_map(
        shards,
        mesh=mesh,
        in_specs=placed,
        out_specs=(P("row", "col", None), P(), P(), P(), P(), P(), P(), P()),
        check_vma=False,
    )
```

```python
import functools
import math

import jax
import jax.numpy as jnp
from jax import lax
from jax.experimental import pallas as pl
from jax.experimental.pallas import tpu as pltpu
from jax.sharding import PartitionSpec as P

EPSILON = 1e-05


def normalize(rows_in, ln_gain, ln_bias):
    values = rows_in.astype(jnp.float32)
    centered = values - jnp.mean(values, axis=-1, keepdims=True)
    variance = jnp.mean(centered * centered, axis=-1, keepdims=True)
    unit_rows = centered * lax.rsqrt(variance + EPSILON)
    normed = (unit_rows * ln_gain + ln_bias).astype(jnp.bfloat16)
    return (unit_rows, normed)


def inner(left, right):
    return lax.dot_general(
        left, right, (((0,), (0,)), ((), ())), preferred_element_type=jnp.float32
    )


def advance(rows_in, ln_gain, ln_bias, gate_weight, up_weight, out_weight):
    unit_rows, normed = normalize(rows_in, ln_gain, ln_bias)
    gate_pre = jnp.dot(normed, gate_weight, preferred_element_type=jnp.float32)
    up_pre = jnp.dot(normed, up_weight, preferred_element_type=jnp.float32)
    hidden = (jax.nn.silu(gate_pre) * up_pre).astype(jnp.bfloat16)
    update = jnp.dot(hidden, out_weight, preferred_element_type=jnp.float32)
    return (rows_in.astype(jnp.float32) + update).astype(jnp.bfloat16)


def against(left, right):
    return lax.dot_general(
        left, right, (((1,), (1,)), ((), ())), preferred_element_type=jnp.float32
    )


def retreat(rows_in, grad_rows, ln_gain, ln_bias, gate_weight, up_weight, out_weight):
    unit_rows, normed = normalize(rows_in, ln_gain, ln_bias)
    gate_pre = jnp.dot(normed, gate_weight, preferred_element_type=jnp.float32)
    up_pre = jnp.dot(normed, up_weight, preferred_element_type=jnp.float32)
    squashed = jax.nn.sigmoid(gate_pre)
    silu_val = gate_pre * squashed
    hidden = (silu_val * up_pre).astype(jnp.bfloat16)
    grad_hidden = against(grad_rows, out_weight)
    grad_gate_pre = (grad_hidden * up_pre * squashed * (1.0 + gate_pre * (1.0 - squashed))).astype(
        jnp.bfloat16
    )
    grad_up_pre = (grad_hidden * silu_val).astype(jnp.bfloat16)
    grad_normed = against(grad_gate_pre, gate_weight) + against(grad_up_pre, up_weight)
    return (
        jnp.sum(grad_normed * unit_rows, axis=0, keepdims=True),
        jnp.sum(grad_normed, axis=0, keepdims=True),
        inner(normed, grad_gate_pre),
        inner(normed, grad_up_pre),
        inner(grad_rows, hidden),
    )


def flip_bit(axis, bit):
    place = lax.axis_index(axis)
    mine = lax.rem(lax.div(place, bit), 2)
    return mine, place + bit - 2 * bit * mine


def total_kernel(bits, parts, shapes, *refs):
    count = len(shapes)
    ins, outs = refs[:count], refs[count : 2 * count]
    acc, full, send_sem, recv_sem = refs[2 * count : 2 * count + 4]
    landing = refs[2 * count + 4 :]
    steps = len(bits)
    barrier = pltpu.get_barrier_semaphore()
    sides = []
    for axis, bit in bits:
        mine, partner = flip_bit(axis, bit)
        sides.append((mine, {axis: partner}))
        pl.semaphore_signal(
            barrier, inc=1, device_id={axis: partner}, device_id_type=pl.DeviceIdType.MESH
        )
    row = 0
    for ref, shape in zip(ins, shapes):
        for left in range(0, shape[1], 128):
            wide = min(128, shape[1] - left)
            acc[row : row + shape[0], :wide] = ref[:, left : left + wide]
            if wide < 128:
                acc[row : row + shape[0], wide:] = jnp.zeros((shape[0], 128 - wide), jnp.float32)
            row += shape[0]
    if row < acc.shape[0]:
        acc[row:, :] = jnp.zeros((acc.shape[0] - row, 128), jnp.float32)
    pl.semaphore_wait(barrier, steps)

    def push(part, slot, source, target, device):
        return pltpu.make_async_remote_copy(
            src_ref=source,
            dst_ref=target,
            send_sem=send_sem.at[part, slot],
            recv_sem=recv_sem.at[part, slot],
            device_id=device,
            device_id_type=pl.DeviceIdType.MESH,
        )

    spots = [(base, size) for base, size, order in parts]
    trail = [[] for part in parts]
    for step in range(steps):
        moves = []
        for index, (base, size, order) in enumerate(parts):
            mine, device = sides[order[step]]
            start, length = spots[index]
            land = landing[index * steps + step]
            if step < steps - 1:
                length //= 2
                keep = pl.multiple_of(start + mine * length, 8)
                give = pl.multiple_of(start + (1 - mine) * length, 8)
                trail[index].append((keep, length, order[step]))
            else:
                keep = give = start
            copy = push(index, step, acc.at[pl.ds(give, length)], land, device)
            copy.start()
            moves.append((copy, keep, length, land))
            spots[index] = (keep, length)
        for copy, keep, length, land in moves:
            copy.wait()
            into = acc if step < steps - 1 else full
            into[pl.ds(keep, length), :] = acc[pl.ds(keep, length), :] + land[...]
    for step in range(steps - 2, -1, -1):
        moves = []
        for index, (base, size, order) in enumerate(parts):
            keep, length, which = trail[index][step]
            spot = full.at[pl.ds(keep, length)]
            copy = push(index, 2 * steps - 2 - step, spot, spot, sides[which][1])
            copy.start()
            moves.append(copy)
        for copy in moves:
            copy.wait()
    row = 0
    for ref, shape in zip(outs, shapes):
        for left in range(0, shape[1], 128):
            wide = min(128, shape[1] - left)
            ref[:, left : left + wide] = full[row : row + shape[0], :wide]
            row += shape[0]


def total(arrays):
    bits = []
    for axis in ("row", "col"):
        size, bit = lax.axis_size(axis), 1
        if size & (size - 1):
            return lax.psum(arrays, ("row", "col"))
        while bit < size:
            bits.append((axis, bit))
            bit *= 2
    if len(bits) < 2:
        return lax.psum(arrays, ("row", "col"))
    shapes = tuple(array.shape for array in arrays)
    rows = sum(shape[0] * (-(-shape[1] // 128)) for shape in shapes)
    steps = len(bits)
    grain = 8 * 2 ** (steps - 1)
    grains = -(-rows // grain)
    inner_bits = list(range(1, steps - 1))
    turns = max(1, min(3, len(inner_bits), grains))
    parts, base = [], 0
    for turn in range(turns):
        size = grain * (grains // turns + (turn < grains % turns))
        order = [0] + inner_bits[turn:] + inner_bits[:turn] + [steps - 1]
        parts.append((base, size, order))
        base += size
    landing = []
    for base_at, size, order in parts:
        for step in range(steps):
            landing.append(
                pltpu.VMEM((size >> min(step + 1, steps - 1), 128), jnp.float32)
            )
    vmem = pl.BlockSpec(memory_space=pltpu.VMEM)
    return pl.pallas_call(
        functools.partial(total_kernel, bits, parts, shapes),
        out_shape=[jax.ShapeDtypeStruct(shape, jnp.float32) for shape in shapes],
        in_specs=[vmem] * len(shapes),
        out_specs=[vmem] * len(shapes),
        scratch_shapes=[
            pltpu.VMEM((base, 128), jnp.float32),
            pltpu.VMEM((base, 128), jnp.float32),
            pltpu.SemaphoreType.DMA((turns, 2 * steps - 1)),
            pltpu.SemaphoreType.DMA((turns, 2 * steps - 1)),
        ]
        + landing,
        compiler_params=pltpu.CompilerParams(
            collective_id=0, has_side_effects=True, vmem_limit_bytes=32 * 1024 * 1024
        ),
        name="total",
    )(*arrays)


def forward_kernel(
    pair_ref, gain_ref, bias_ref, gate_ref, up_ref, out_ref, both_ref, *results
):
    rows_ref, packed_ref = results
    shape = pair_ref.shape
    rows_out = advance(
        pair_ref[...].reshape(-1, shape[3]),
        gain_ref[...],
        bias_ref[...],
        gate_ref[...],
        up_ref[...],
        out_ref[...],
    )
    rows_ref[...] = rows_out.reshape(shape)
    middle = rows_out.shape[0] // 2
    wide = jnp.concatenate([rows_out[:middle], rows_out[middle:]], axis=1)
    packed = jnp.dot(wide, both_ref[...], preferred_element_type=jnp.float32)
    packed_ref[...] = packed.astype(jnp.bfloat16).reshape(packed_ref.shape)


def forward(piece, pieces, pair, gain, bias, gate_weight, up_weight, out_weight, head_weight):
    rows_tile, cols_tile, width = pair.shape
    bins = head_weight.shape[1]
    deep = rows_tile // pieces
    group = math.gcd(deep // 2, max(1, 512 // cols_tile))
    empty = jnp.zeros_like(head_weight)
    both = jnp.concatenate(
        [
            jnp.concatenate([head_weight, empty], axis=1),
            jnp.concatenate([empty, head_weight], axis=1),
        ]
    )
    def whole(array):
        return pl.BlockSpec(array.shape, lambda step: (0, 0))

    split = pair.reshape(2 * pieces, deep // 2, cols_tile, width)
    weights = [gain[None], bias[None], gate_weight, up_weight, out_weight, both]
    rows_out, packed = pl.pallas_call(
        forward_kernel,
        grid=(deep // 2 // group,),
        out_shape=[
            jax.ShapeDtypeStruct((2, deep // 2, cols_tile, width), jnp.bfloat16),
            jax.ShapeDtypeStruct((deep // 2, cols_tile, 2 * bins), jnp.bfloat16),
        ],
        in_specs=[
            pl.BlockSpec((2, group, cols_tile, width), lambda step: (piece, step, 0, 0))
        ]
        + [whole(array) for array in weights],
        out_specs=[
            pl.BlockSpec((2, group, cols_tile, width), lambda step: (0, step, 0, 0)),
            pl.BlockSpec((group, cols_tile, 2 * bins), lambda step: (step, 0, 0)),
        ],
        compiler_params=pltpu.CompilerParams(vmem_limit_bytes=32 * 1024 * 1024),
        cost_estimate=pl.CostEstimate(
            flops=6 * deep * cols_tile * width * gate_weight.shape[1],
            bytes_accessed=6 * deep * cols_tile * width,
            transcendentals=deep * cols_tile * gate_weight.shape[1],
        ),
        name="forward",
    )(split, *weights)
    return (
        rows_out.reshape(deep, cols_tile, width),
        packed,
    )


def mirror(packed_part):
    across, down = lax.axis_size("row"), lax.axis_size("col")
    fold = across // down
    deep, cols_tile, bins = packed_part.shape
    edge = cols_tile // fold
    place = lax.axis_index("row")
    came = []
    for turn in range(fold):
        sub = lax.rem(place + turn, fold)
        packed = lax.dynamic_slice(packed_part, (0, sub * edge, 0), (deep, edge, bins))
        pairs = [
            (r * down + c, (c * fold + (r + turn) % fold) * down + r // fold)
            for r in range(across)
            for c in range(down)
        ]
        came.append(lax.ppermute(packed, ("row", "col"), pairs))
    return came


def ordered(came):
    fold = len(came)
    place = lax.axis_index("row")
    stacked = jnp.stack(came)
    return jnp.concatenate(
        [
            lax.dynamic_slice_in_dim(stacked, lax.rem(place + fold - sub, fold), 1)
            for sub in range(fold)
        ]
    )


def backward_kernel(tokens, *refs):
    pair_ref, rows_ref, flip_ref, code_ref, turn_ref = refs[:5]
    gain_ref, bias_ref, gate_ref, up_ref, out_ref, head_ref = refs[5:11]
    before, after = refs[11:16], refs[16:21]

    @pl.when((pl.program_id(0) == 0) & (pl.program_id(1) == 0))
    def start():
        for old, new in zip(before, after):
            new[...] = old[...]

    shape = pair_ref.shape
    bins = head_ref.shape[1]
    rows_in = pair_ref[...].reshape(-1, shape[3])
    rows_out = rows_ref[...].reshape(-1, shape[3])
    half = jnp.dot(rows_out, head_ref[...], preferred_element_type=jnp.float32)
    half = half.astype(jnp.bfloat16).astype(jnp.float32)
    packed = jnp.swapaxes(flip_ref[0].astype(jnp.float32), 0, 1)
    flipped = jnp.concatenate([packed[..., :bins], packed[..., bins:]], axis=1)
    logits = half.reshape(flipped.shape) + flipped
    bin_at = lax.broadcasted_iota(jnp.int32, logits.shape, 2)
    log_total = jnp.log(jnp.sum(jnp.exp(logits), axis=-1, keepdims=True))
    soft_probs = jnp.exp(logits - log_total)

    def split(ref):
        codes = lax.broadcast_in_dim(ref[0], logits.shape, (0, 1))
        hot = (codes == bin_at).astype(jnp.float32)
        return hot, (codes >= 0).astype(jnp.float32)

    hot, mask = split(code_ref)
    hot_turn, mask_turn = split(turn_ref)
    loss_rows = mask[..., :1] * (log_total - jnp.sum(logits * hot, axis=-1, keepdims=True))
    tile_grad = (mask * (soft_probs - hot) / tokens).astype(jnp.bfloat16)
    tile_flip = (mask_turn * (soft_probs - hot_turn) / tokens).astype(jnp.bfloat16)
    both = jnp.concatenate([tile_grad.reshape(-1, bins), tile_flip.reshape(-1, bins)], axis=1)
    head = head_ref[...]
    grad_rows = against(both, jnp.concatenate([head, head], axis=1)).astype(jnp.bfloat16)
    gain_sum, bias_sum, gate_sum, up_sum, out_sum = retreat(
        rows_in, grad_rows, gain_ref[...], bias_ref[...], gate_ref[...], up_ref[...], out_ref[...]
    )
    after[0][...] += gate_sum
    after[1][...] += up_sum
    after[2][...] += out_sum
    after[3][...] += inner(rows_out, both)
    few = after[4]
    few[0:1, :] += gain_sum
    few[1:2, :] += bias_sum
    few[2:3, :] += jnp.broadcast_to(jnp.sum(loss_rows), gain_sum.shape)


def backward(
    piece, pieces, tokens, totals, pair, pair_out, flips, codes, turns, weights
):
    rows_tile, cols_tile, width = pair.shape
    fold = flips.shape[0]
    deep = cols_tile // (fold * pieces)
    group = math.gcd(rows_tile, max(8, 1024 // deep))

    def whole(array):
        return pl.BlockSpec(array.shape, lambda sub, step: (0, 0))

    tile = pl.BlockSpec(
        (group, 1, deep, width), lambda sub, step: (step, sub * pieces + piece, 0, 0)
    )
    code = pl.BlockSpec((1, group, deep), lambda sub, step: (sub * pieces + piece, step, 0))
    flip = pl.BlockSpec(
        (1, deep // 2, group, flips.shape[3]), lambda sub, step: (sub, 0, step, 0)
    )
    cut = (rows_tile, fold * pieces, deep, width)
    return pl.pallas_call(
        functools.partial(backward_kernel, tokens),
        grid=(fold, rows_tile // group),
        out_shape=[jax.ShapeDtypeStruct(array.shape, jnp.float32) for array in totals],
        in_specs=[tile, tile, flip, code, code]
        + [whole(array) for array in weights]
        + [whole(array) for array in totals],
        out_specs=[whole(array) for array in totals],
        compiler_params=pltpu.CompilerParams(vmem_limit_bytes=48 * 1024 * 1024),
        cost_estimate=pl.CostEstimate(
            flops=16 * rows_tile * deep * fold * width * weights[2].shape[1],
            bytes_accessed=8 * rows_tile * deep * fold * width,
            transcendentals=rows_tile * deep * fold * weights[2].shape[1],
        ),
        name="backward",
    )(pair.reshape(cut), pair_out.reshape(cut), flips, codes, turns, *weights, *totals)


def shards(
    pair, ln_gain, ln_bias, gate_weight, up_weight, out_weight, head_weight, targets, pair_mask
):
    rows_tile, cols_tile, width = pair.shape
    bins = head_weight.shape[1]
    tokens = cols_tile * lax.axis_size("col")
    fold = lax.axis_size("row") // lax.axis_size("col")
    pieces = 2
    deep = rows_tile // pieces

    code = jnp.where(pair_mask > 0, targets, -1)
    codes = lax.all_gather(code, ("row", "col"), axis=0, tiled=True)
    top, side = lax.axis_index("row") * rows_tile, lax.axis_index("col") * cols_tile
    code_tile = lax.dynamic_slice(codes, (top, side), (rows_tile, cols_tile))
    code_turn = lax.dynamic_slice(codes, (side, top), (cols_tile, rows_tile)).T

    outs, arrivals = [], []
    for piece in range(pieces):
        rows_out, packed = forward(
            piece, pieces, pair, ln_gain, ln_bias, gate_weight, up_weight, out_weight, head_weight
        )
        outs.append(rows_out)
        arrivals.append(mirror(packed))
    pair_out = jnp.concatenate(outs)

    def by_columns(array):
        return jnp.swapaxes(array.reshape(rows_tile, fold * pieces, deep), 0, 1)

    hidden_width = gate_weight.shape[1]
    totals = [
        jnp.zeros((width, hidden_width), jnp.float32),
        jnp.zeros((width, hidden_width), jnp.float32),
        jnp.zeros((width, hidden_width), jnp.float32),
        jnp.zeros((width, 2 * bins), jnp.float32),
        jnp.zeros((8, width), jnp.float32),
    ]
    weights = [ln_gain[None], ln_bias[None], gate_weight, up_weight, out_weight, head_weight]
    codes_here, codes_turn = by_columns(code_tile), by_columns(code_turn)
    for piece in range(pieces):
        totals = backward(
            piece,
            pieces,
            tokens,
            totals,
            pair,
            pair_out,
            ordered(arrivals[piece]),
            codes_here,
            codes_turn,
            weights,
        )
    gate_sum, up_sum, out_sum, head_sum, few = total(list(totals))
    head_sum = head_sum[:, :bins] + head_sum[:, bins:]
    out_sum = out_sum.T
    loss = few[2, 0] / (tokens * tokens)
    return (pair_out, loss, few[0], few[1], gate_sum, up_sum, out_sum, head_sum)


def solution(mesh):
    placed = (
        P("row", "col", None),
        P(),
        P(),
        P(),
        P(),
        P(),
        P(),
        P(("row", "col"), None),
        P(("row", "col"), None),
    )
    return jax.shard_map(
        shards,
        mesh=mesh,
        in_specs=placed,
        out_specs=(P("row", "col", None), P(), P(), P(), P(), P(), P(), P()),
        check_vma=False,
    )
```

```python
import functools
import math

import jax
import jax.numpy as jnp
from jax import lax
from jax.experimental import pallas as pl
from jax.experimental.pallas import tpu as pltpu
from jax.sharding import PartitionSpec as P

EPSILON = 1e-05


def normalize(rows_in, ln_gain, ln_bias):
    values = rows_in.astype(jnp.float32)
    centered = values - jnp.mean(values, axis=-1, keepdims=True)
    variance = jnp.mean(centered * centered, axis=-1, keepdims=True)
    unit_rows = centered * lax.rsqrt(variance + EPSILON)
    normed = (unit_rows * ln_gain + ln_bias).astype(jnp.bfloat16)
    return (unit_rows, normed)


def inner(left, right):
    return lax.dot_general(
        left, right, (((0,), (0,)), ((), ())), preferred_element_type=jnp.float32
    )


def advance(rows_in, ln_gain, ln_bias, gate_weight, up_weight, out_weight):
    unit_rows, normed = normalize(rows_in, ln_gain, ln_bias)
    gate_pre = jnp.dot(normed, gate_weight, preferred_element_type=jnp.float32)
    up_pre = jnp.dot(normed, up_weight, preferred_element_type=jnp.float32)
    hidden = (jax.nn.silu(gate_pre) * up_pre).astype(jnp.bfloat16)
    update = jnp.dot(hidden, out_weight, preferred_element_type=jnp.float32)
    return (rows_in.astype(jnp.float32) + update).astype(jnp.bfloat16)


def against(left, right):
    return lax.dot_general(
        left, right, (((1,), (1,)), ((), ())), preferred_element_type=jnp.float32
    )


def retreat(rows_in, grad_rows, ln_gain, ln_bias, gate_weight, up_weight, out_weight):
    unit_rows, normed = normalize(rows_in, ln_gain, ln_bias)
    gate_pre = jnp.dot(normed, gate_weight, preferred_element_type=jnp.float32)
    up_pre = jnp.dot(normed, up_weight, preferred_element_type=jnp.float32)
    squashed = jax.nn.sigmoid(gate_pre)
    silu_val = gate_pre * squashed
    hidden = (silu_val * up_pre).astype(jnp.bfloat16)
    grad_hidden = against(grad_rows, out_weight)
    grad_gate_pre = (grad_hidden * up_pre * squashed * (1.0 + gate_pre * (1.0 - squashed))).astype(
        jnp.bfloat16
    )
    grad_up_pre = (grad_hidden * silu_val).astype(jnp.bfloat16)
    grad_normed = against(grad_gate_pre, gate_weight) + against(grad_up_pre, up_weight)
    return (
        jnp.sum(grad_normed * unit_rows, axis=0, keepdims=True),
        jnp.sum(grad_normed, axis=0, keepdims=True),
        inner(normed, grad_gate_pre),
        inner(normed, grad_up_pre),
        inner(grad_rows, hidden),
    )


def flip_bit(axis, bit):
    place = lax.axis_index(axis)
    mine = lax.rem(lax.div(place, bit), 2)
    return mine, place + bit - 2 * bit * mine


def total_kernel(bits, parts, shapes, *refs):
    count = len(shapes)
    ins, outs = refs[:count], refs[count : 2 * count]
    acc, full, send_sem, recv_sem = refs[2 * count : 2 * count + 4]
    landing = refs[2 * count + 4 :]
    steps = len(bits)
    barrier = pltpu.get_barrier_semaphore()
    sides = []
    for axis, bit in bits:
        mine, partner = flip_bit(axis, bit)
        sides.append((mine, {axis: partner}))
        pl.semaphore_signal(
            barrier, inc=1, device_id={axis: partner}, device_id_type=pl.DeviceIdType.MESH
        )
    row = 0
    for ref, shape in zip(ins, shapes):
        for left in range(0, shape[1], 128):
            wide = min(128, shape[1] - left)
            acc[row : row + shape[0], :wide] = ref[:, left : left + wide]
            if wide < 128:
                acc[row : row + shape[0], wide:] = jnp.zeros((shape[0], 128 - wide), jnp.float32)
            row += shape[0]
    if row < acc.shape[0]:
        acc[row:, :] = jnp.zeros((acc.shape[0] - row, 128), jnp.float32)
    pl.semaphore_wait(barrier, steps)

    def push(part, slot, source, target, device):
        return pltpu.make_async_remote_copy(
            src_ref=source,
            dst_ref=target,
            send_sem=send_sem.at[part, slot],
            recv_sem=recv_sem.at[part, slot],
            device_id=device,
            device_id_type=pl.DeviceIdType.MESH,
        )

    spots = [(base, size) for base, size, order in parts]
    trail = [[] for part in parts]
    for step in range(steps):
        moves = []
        for index, (base, size, order) in enumerate(parts):
            mine, device = sides[order[step]]
            start, length = spots[index]
            land = landing[index * steps + step]
            if step < steps - 1:
                length //= 2
                keep = pl.multiple_of(start + mine * length, 8)
                give = pl.multiple_of(start + (1 - mine) * length, 8)
                trail[index].append((keep, length, order[step]))
            else:
                keep = give = start
            copy = push(index, step, acc.at[pl.ds(give, length)], land, device)
            copy.start()
            moves.append((copy, keep, length, land))
            spots[index] = (keep, length)
        for copy, keep, length, land in moves:
            copy.wait()
            into = acc if step < steps - 1 else full
            into[pl.ds(keep, length), :] = acc[pl.ds(keep, length), :] + land[...]
    for step in range(steps - 2, -1, -1):
        moves = []
        for index, (base, size, order) in enumerate(parts):
            keep, length, which = trail[index][step]
            spot = full.at[pl.ds(keep, length)]
            copy = push(index, 2 * steps - 2 - step, spot, spot, sides[which][1])
            copy.start()
            moves.append(copy)
        for copy in moves:
            copy.wait()
    row = 0
    for ref, shape in zip(outs, shapes):
        for left in range(0, shape[1], 128):
            wide = min(128, shape[1] - left)
            ref[:, left : left + wide] = full[row : row + shape[0], :wide]
            row += shape[0]


def total(arrays):
    bits = []
    for axis in ("row", "col"):
        size, bit = lax.axis_size(axis), 1
        if size & (size - 1):
            return lax.psum(arrays, ("row", "col"))
        while bit < size:
            bits.append((axis, bit))
            bit *= 2
    if len(bits) < 2:
        return lax.psum(arrays, ("row", "col"))
    shapes = tuple(array.shape for array in arrays)
    rows = sum(shape[0] * (-(-shape[1] // 128)) for shape in shapes)
    steps = len(bits)
    grain = 8 * 2 ** (steps - 1)
    grains = -(-rows // grain)
    inner_bits = list(range(1, steps - 1))
    turns = max(1, min(3, len(inner_bits), grains))
    parts, base = [], 0
    for turn in range(turns):
        size = grain * (grains // turns + (turn < grains % turns))
        order = [0] + inner_bits[turn:] + inner_bits[:turn] + [steps - 1]
        parts.append((base, size, order))
        base += size
    landing = []
    for base_at, size, order in parts:
        for step in range(steps):
            landing.append(
                pltpu.VMEM((size >> min(step + 1, steps - 1), 128), jnp.float32)
            )
    vmem = pl.BlockSpec(memory_space=pltpu.VMEM)
    return pl.pallas_call(
        functools.partial(total_kernel, bits, parts, shapes),
        out_shape=[jax.ShapeDtypeStruct(shape, jnp.float32) for shape in shapes],
        in_specs=[vmem] * len(shapes),
        out_specs=[vmem] * len(shapes),
        scratch_shapes=[
            pltpu.VMEM((base, 128), jnp.float32),
            pltpu.VMEM((base, 128), jnp.float32),
            pltpu.SemaphoreType.DMA((turns, 2 * steps - 1)),
            pltpu.SemaphoreType.DMA((turns, 2 * steps - 1)),
        ]
        + landing,
        compiler_params=pltpu.CompilerParams(
            collective_id=0, has_side_effects=True, vmem_limit_bytes=32 * 1024 * 1024
        ),
        name="total",
    )(*arrays)


def forward_kernel(
    pair_ref, gain_ref, bias_ref, gate_ref, up_ref, out_ref, both_ref, *results
):
    rows_ref, packed_ref = results
    shape = pair_ref.shape
    rows_out = advance(
        pair_ref[...].reshape(-1, shape[3]),
        gain_ref[...],
        bias_ref[...],
        gate_ref[...],
        up_ref[...],
        out_ref[...],
    )
    rows_ref[...] = rows_out.reshape(shape)
    middle = rows_out.shape[0] // 2
    wide = jnp.concatenate([rows_out[:middle], rows_out[middle:]], axis=1)
    packed = jnp.dot(wide, both_ref[...], preferred_element_type=jnp.float32)
    packed_ref[...] = packed.astype(jnp.bfloat16).reshape(packed_ref.shape)


def forward(piece, pieces, pair, gain, bias, gate_weight, up_weight, out_weight, head_weight):
    rows_tile, cols_tile, width = pair.shape
    bins = head_weight.shape[1]
    deep = rows_tile // pieces
    group = math.gcd(deep // 2, max(1, 512 // cols_tile))
    empty = jnp.zeros_like(head_weight)
    both = jnp.concatenate(
        [
            jnp.concatenate([head_weight, empty], axis=1),
            jnp.concatenate([empty, head_weight], axis=1),
        ]
    )
    def whole(array):
        return pl.BlockSpec(array.shape, lambda step: (0, 0))

    split = pair.reshape(2 * pieces, deep // 2, cols_tile, width)
    weights = [gain[None], bias[None], gate_weight, up_weight, out_weight, both]
    rows_out, packed = pl.pallas_call(
        forward_kernel,
        grid=(deep // 2 // group,),
        out_shape=[
            jax.ShapeDtypeStruct((2, deep // 2, cols_tile, width), jnp.bfloat16),
            jax.ShapeDtypeStruct((deep // 2, cols_tile, 2 * bins), jnp.bfloat16),
        ],
        in_specs=[
            pl.BlockSpec((2, group, cols_tile, width), lambda step: (piece, step, 0, 0))
        ]
        + [whole(array) for array in weights],
        out_specs=[
            pl.BlockSpec((2, group, cols_tile, width), lambda step: (0, step, 0, 0)),
            pl.BlockSpec((group, cols_tile, 2 * bins), lambda step: (step, 0, 0)),
        ],
        compiler_params=pltpu.CompilerParams(vmem_limit_bytes=32 * 1024 * 1024),
        cost_estimate=pl.CostEstimate(
            flops=6 * deep * cols_tile * width * gate_weight.shape[1],
            bytes_accessed=6 * deep * cols_tile * width,
            transcendentals=deep * cols_tile * gate_weight.shape[1],
        ),
        name="forward",
    )(split, *weights)
    return (
        rows_out.reshape(deep, cols_tile, width),
        packed,
    )


def mirror(packed_part):
    across, down = lax.axis_size("row"), lax.axis_size("col")
    fold = across // down
    edge = packed_part.shape[1] // fold
    place = lax.axis_index("row")
    came = []
    for turn in range(fold):
        sub = lax.rem(place + turn, fold)
        packed = lax.dynamic_slice_in_dim(packed_part, sub * edge, edge, 1)
        pairs = [
            (r * down + c, (c * fold + (r + turn) % fold) * down + r // fold)
            for r in range(across)
            for c in range(down)
        ]
        came.append(lax.ppermute(packed, ("row", "col"), pairs))
    return came


def ordered(came):
    fold = len(came)
    place = lax.axis_index("row")
    stacked = jnp.stack(came)
    return jnp.concatenate(
        [
            lax.dynamic_slice_in_dim(stacked, lax.rem(place + fold - sub, fold), 1)
            for sub in range(fold)
        ]
    )


def backward_kernel(tokens, *refs):
    pair_ref, rows_ref, flip_ref, code_ref, turn_ref = refs[:5]
    gain_ref, bias_ref, gate_ref, up_ref, out_ref, head_ref = refs[5:11]
    before, after = refs[11:16], refs[16:21]

    @pl.when((pl.program_id(0) == 0) & (pl.program_id(1) == 0))
    def start():
        for old, new in zip(before, after):
            new[...] = old[...]

    shape = pair_ref.shape
    bins = head_ref.shape[1]
    rows_in = pair_ref[...].reshape(-1, shape[3])
    rows_out = rows_ref[...].reshape(-1, shape[3])
    half = jnp.dot(rows_out, head_ref[...], preferred_element_type=jnp.float32)
    half = half.astype(jnp.bfloat16).astype(jnp.float32)
    packed = jnp.swapaxes(flip_ref[0].astype(jnp.float32), 0, 1)
    flipped = jnp.concatenate([packed[..., :bins], packed[..., bins:]], axis=1)
    logits = half.reshape(flipped.shape) + flipped
    bin_at = lax.broadcasted_iota(jnp.int32, logits.shape, 2)
    log_total = jnp.log(jnp.sum(jnp.exp(logits), axis=-1, keepdims=True))
    soft_probs = jnp.exp(logits - log_total)

    def split(ref):
        codes = lax.broadcast_in_dim(ref[0], logits.shape, (0, 1))
        hot = (codes == bin_at).astype(jnp.float32)
        return hot, (codes >= 0).astype(jnp.float32)

    hot, mask = split(code_ref)
    hot_turn, mask_turn = split(turn_ref)
    loss_rows = mask[..., :1] * (log_total - jnp.sum(logits * hot, axis=-1, keepdims=True))
    tile_grad = (mask * (soft_probs - hot) / tokens).astype(jnp.bfloat16)
    tile_flip = (mask_turn * (soft_probs - hot_turn) / tokens).astype(jnp.bfloat16)
    both = jnp.concatenate([tile_grad.reshape(-1, bins), tile_flip.reshape(-1, bins)], axis=1)
    head = head_ref[...]
    grad_rows = against(both, jnp.concatenate([head, head], axis=1)).astype(jnp.bfloat16)
    gain_sum, bias_sum, gate_sum, up_sum, out_sum = retreat(
        rows_in, grad_rows, gain_ref[...], bias_ref[...], gate_ref[...], up_ref[...], out_ref[...]
    )
    after[0][...] += gate_sum
    after[1][...] += up_sum
    after[2][...] += out_sum
    after[3][...] += inner(rows_out, both)
    few = after[4]
    few[0:1, :] += gain_sum
    few[1:2, :] += bias_sum
    few[2:3, :] += jnp.broadcast_to(jnp.sum(loss_rows), gain_sum.shape)


def backward(
    piece, pieces, tokens, totals, pair, pair_out, flips, codes, turns, weights
):
    rows_tile, cols_tile, width = pair.shape
    fold = flips.shape[0]
    deep = cols_tile // (fold * pieces)
    group = math.gcd(rows_tile, max(8, 1024 // deep))

    def whole(array):
        return pl.BlockSpec(array.shape, lambda sub, step: (0, 0))

    tile = pl.BlockSpec(
        (group, 1, deep, width), lambda sub, step: (step, sub * pieces + piece, 0, 0)
    )
    code = pl.BlockSpec((1, group, deep), lambda sub, step: (sub * pieces + piece, step, 0))
    flip = pl.BlockSpec(
        (1, deep // 2, group, flips.shape[3]), lambda sub, step: (sub, 0, step, 0)
    )
    cut = (rows_tile, fold * pieces, deep, width)
    return pl.pallas_call(
        functools.partial(backward_kernel, tokens),
        grid=(fold, rows_tile // group),
        out_shape=[jax.ShapeDtypeStruct(array.shape, jnp.float32) for array in totals],
        in_specs=[tile, tile, flip, code, code]
        + [whole(array) for array in weights]
        + [whole(array) for array in totals],
        out_specs=[whole(array) for array in totals],
        compiler_params=pltpu.CompilerParams(vmem_limit_bytes=48 * 1024 * 1024),
        cost_estimate=pl.CostEstimate(
            flops=16 * rows_tile * deep * fold * width * weights[2].shape[1],
            bytes_accessed=8 * rows_tile * deep * fold * width,
            transcendentals=rows_tile * deep * fold * weights[2].shape[1],
        ),
        name="backward",
    )(pair.reshape(cut), pair_out.reshape(cut), flips, codes, turns, *weights, *totals)


def shards(
    pair, ln_gain, ln_bias, gate_weight, up_weight, out_weight, head_weight, targets, pair_mask
):
    rows_tile, cols_tile, width = pair.shape
    bins = head_weight.shape[1]
    tokens = cols_tile * lax.axis_size("col")
    fold = lax.axis_size("row") // lax.axis_size("col")
    pieces = 2
    deep = rows_tile // pieces

    code = jnp.where(pair_mask > 0, targets, -1)
    code_tile = lax.all_to_all(code, "col", split_axis=1, concat_axis=0, tiled=True)
    turned = jnp.swapaxes(ordered(mirror(code_tile)), 1, 2)

    outs, arrivals = [], []
    for piece in range(pieces):
        rows_out, packed = forward(
            piece, pieces, pair, ln_gain, ln_bias, gate_weight, up_weight, out_weight, head_weight
        )
        outs.append(rows_out)
        arrivals.append(mirror(packed))
    pair_out = jnp.concatenate(outs)

    def by_columns(array):
        return jnp.swapaxes(array.reshape(rows_tile, fold * pieces, deep), 0, 1)

    hidden_width = gate_weight.shape[1]
    totals = [
        jnp.zeros((width, hidden_width), jnp.float32),
        jnp.zeros((width, hidden_width), jnp.float32),
        jnp.zeros((width, hidden_width), jnp.float32),
        jnp.zeros((width, 2 * bins), jnp.float32),
        jnp.zeros((8, width), jnp.float32),
    ]
    weights = [ln_gain[None], ln_bias[None], gate_weight, up_weight, out_weight, head_weight]
    codes_here = by_columns(code_tile)
    codes_turn = jnp.swapaxes(turned.reshape(fold, rows_tile, pieces, deep), 1, 2)
    codes_turn = codes_turn.reshape(fold * pieces, rows_tile, deep)
    for piece in range(pieces):
        totals = backward(
            piece,
            pieces,
            tokens,
            totals,
            pair,
            pair_out,
            ordered(arrivals[piece]),
            codes_here,
            codes_turn,
            weights,
        )
    gate_sum, up_sum, out_sum, head_sum, few = total(list(totals))
    head_sum = head_sum[:, :bins] + head_sum[:, bins:]
    out_sum = out_sum.T
    loss = few[2, 0] / (tokens * tokens)
    return (pair_out, loss, few[0], few[1], gate_sum, up_sum, out_sum, head_sum)


def solution(mesh):
    placed = (
        P("row", "col", None),
        P(),
        P(),
        P(),
        P(),
        P(),
        P(),
        P(("row", "col"), None),
        P(("row", "col"), None),
    )
    return jax.shard_map(
        shards,
        mesh=mesh,
        in_specs=placed,
        out_specs=(P("row", "col", None), P(), P(), P(), P(), P(), P(), P()),
        check_vma=False,
    )
```
